32 devices in a mesh: ctx: 8 (over z, y), wt: 4 (over x, core).
Axes of the slice: x: 2, y: 2, z: 4, core: 2. Of those that a mesh axis runs over, the one named last changes fastest.
Arguments:
- frames: bfloat16 [512, 1280], P('wt'), may hold values from -6 to 6
- span_source: int32 [32], P('wt'), may hold values from 0 to 7, as said below
- adapter_weight: bfloat16 [1280, 4096], P(None, 'ctx'), may hold values from -0.15625 to 0.15625
- adapter_bias: float32 [4096], P('ctx'), may hold values from -3 to 3
- norm_gain: float32 [4096], replicated, may hold values from 0.25 to 1.75
- qkv_weight: bfloat16 [4096, 3, 4096], P('wt', None, 'ctx'), may hold values from -0.09375 to 0.09375
- out_weight: bfloat16 [4096, 4096], P('ctx', 'wt'), may hold values from -0.125 to 0.125
- k_cache: bfloat16 [8, 1024, 4096], P('wt', 'ctx'), may hold values from -600 to 600
- v_cache: bfloat16 [8, 1024, 4096], P('wt', 'ctx'), may hold values from -12 to 12
- lengths: int32 [8], P('wt'), may hold values from 1 to 1024
Outputs:
- attn_out: bfloat16 [512, 4096], P('wt', 'ctx')
- new_keys: bfloat16 [512, 4096], P('wt', 'ctx')
- new_values: bfloat16 [512, 4096], P('wt', 'ctx')
The draws below stay inside these ranges and needn't reach their ends.
Inputs may be any that keep to these rules, and one draw needn't show every extreme that they name: `span_source`: each aligned block of 8 entries is a permutation of 0 to 7.
All inputs are finite; a program needn't handle non-finite values.
Results may differ from the reference program's by a relative error of at most 0.02.
Values may be sent and summed in bfloat16 or wider, within the bound.
A program may use at most 64 MiB of HBM per device.

```python
import jax
import jax.numpy as jnp
from jax import lax

D = 4096
HEADS = 32
HEAD = 128
AUDIO = 1280
NEW = 64
SPAN = 16
MEETINGS = 8
TOKENS = 512
HIST = 1024
GROUP_SPANS = 8
SPANS = 32


def draw_span_source(key, part):
    groups = SPANS // GROUP_SPANS
    group_keys = jax.random.split(jax.random.fold_in(key, 11), groups)
    orders = jax.vmap(lambda single: jax.random.permutation(single, GROUP_SPANS))(group_keys)
    return orders.reshape(SPANS).astype(jnp.int32)


def draw_k_cache(key, part):
    base = jax.random.truncated_normal(jax.random.fold_in(key, 21), -6.0, 6.0, (MEETINGS, HIST, D), jnp.float32)
    return base.astype(jnp.bfloat16)


def plant(values, key, low, largest):
    shape = values.shape
    index_at = [jax.random.randint(jax.random.fold_in(key, axis), (), 0, shape[axis]) for axis in range(len(shape))]
    values = values.at[tuple(index_at)].set(low)
    longest = shape.index(max(shape))
    index_at[longest] = (index_at[longest] + 1) % shape[longest]
    return values.at[tuple(index_at)].set(largest)


def raised(result, key, source, target, blocks, factor):
    def block_of(dim):
        return (jnp.arange(result.shape[dim]) // (result.shape[dim] // blocks)).reshape((-1,) + (1,) * (result.ndim - 1 - dim))

    one_side = jax.random.permutation(key, blocks)[block_of(target)]
    second = (block_of(target) + blocks // 2) % blocks
    return jnp.where((block_of(source) == one_side) | (block_of(source) == second), factor * result, result)


def level_of(rng, dims, pieces, low, top_value):
    level, own = 1.0, jax.random.fold_in(rng, 6)
    for position, shards_of in pieces:
        steps = jnp.exp(jax.random.uniform(jax.random.fold_in(own, position), (shards_of,), jnp.float32, low / len(pieces), top_value / len(pieces)))
        level = level * jnp.repeat(steps, dims[position] // shards_of).reshape([-1 if axis == position else 1 for axis in range(len(dims))])
    return level


def scatter_about(key, dims, deviation, most, cuts=(), kind=jnp.bfloat16):
    loudness = level_of(key, dims, cuts, -0.22, 0.18) if cuts else 1.0
    result = jax.random.normal(key, dims, jnp.float32) * deviation * loudness
    return jnp.minimum(jnp.maximum(result, -most), most).astype(kind)


def gaussian_with(rng, shape, width, bound, shards, heavy, kind=jnp.bfloat16):
    result = width * jax.random.normal(rng, shape, jnp.float32)
    if shards:
        result = result * level_of(rng, shape, shards, -0.22, 0.18)
    return jnp.clip(raised(result, jax.random.fold_in(rng, 3), *heavy), -bound, bound).astype(kind)


def setup_inputs(seed: int = 0) -> dict:
    keys = jax.random.split(jax.random.key(seed), 11)
    frames = scatter_about(keys[0], (TOKENS, AUDIO), 1.0, 6.0, ((0, 4),))
    span_source = draw_span_source(jax.random.fold_in(keys[10], 71), 0)
    adapter_weight = scatter_about(keys[2], (AUDIO, D), AUDIO ** -0.5, 0.15625, ((1, 8),))
    adapter_bias = scatter_about(keys[3], (D,), 0.5, 3.0, ((0, 8),), jnp.float32)
    norm_gain = jnp.clip(1.0 + 0.15 * jax.random.normal(keys[4], (D,), jnp.float32), 0.25, 1.75)
    qkv_weight = scatter_about(keys[5], (D, 3, D), D ** -0.5, 0.09375, ((0, 4), (2, 8)))
    out_weight = gaussian_with(keys[6], (D, D), D ** -0.5, 0.125, ((0, 8), (1, 4)), (0, 1, 8, 2.0))
    k_cache = draw_k_cache(jax.random.fold_in(keys[10], 71), 0)
    v_cache = scatter_about(keys[8], (MEETINGS, HIST, D), 2.0, 12.0, ((0, 4), (1, 8)))
    lengths = plant(jax.random.randint(keys[9], (MEETINGS,), 1, HIST + 1), jax.random.fold_in(keys[9], 1), 1, HIST).astype(jnp.int32)
    return dict(frames=frames, span_source=span_source, adapter_weight=adapter_weight, adapter_bias=adapter_bias, norm_gain=norm_gain, qkv_weight=qkv_weight, out_weight=out_weight, k_cache=k_cache, v_cache=v_cache, lengths=lengths)


def rotate(values, positions):
    half = values.shape[-1] // 2
    freq = 10000.0 ** (-2.0 * jnp.arange(half, dtype=jnp.float32) / values.shape[-1])
    angle = positions.astype(jnp.float32)[:, None] * freq[None, :]
    cosine = jnp.cos(angle)[:, None, :]
    sine = jnp.sin(angle)[:, None, :]
    first = values[..., :half]
    second = values[..., half:]
    return jnp.concatenate([first * cosine - second * sine, second * cosine + first * sine], axis=-1)

def attend_one(inputs):
    query, keys_hist, vals_hist, keys_new, vals_new, length = inputs
    scale = HEAD ** (-0.5)
    query_wide = query.astype(jnp.float32)
    score_hist = jnp.einsum('thd,phd->htp', query_wide, keys_hist.astype(jnp.float32)) * scale
    score_new = jnp.einsum('thd,shd->hts', query_wide, keys_new.astype(jnp.float32)) * scale
    live = jnp.arange(HIST, dtype=jnp.int32) < length
    causal = jnp.arange(NEW, dtype=jnp.int32)[:, None] >= jnp.arange(NEW, dtype=jnp.int32)[None, :]
    scores = jnp.concatenate([jnp.where(live[None, None, :], score_hist, -jnp.inf), jnp.where(causal[None, :, :], score_new, -jnp.inf)], axis=-1)
    row_max = lax.optimization_barrier(jnp.max(scores, axis=-1, keepdims=True))
    weights = jnp.exp(scores - row_max)
    row_total = lax.optimization_barrier(jnp.sum(weights, axis=-1))
    rounded = lax.optimization_barrier(weights.astype(jnp.bfloat16)).astype(jnp.float32)
    values_all = jnp.concatenate([vals_hist, vals_new], axis=0).astype(jnp.float32)
    numerator = jnp.einsum('htp,phd->thd', rounded, values_all)
    return (numerator / jnp.transpose(row_total)[:, :, None]).astype(jnp.bfloat16)

def reference(frames, span_source, adapter_weight, adapter_bias, norm_gain, qkv_weight, out_weight, k_cache, v_cache, lengths):
    base = jnp.arange(SPANS, dtype=jnp.int32) // GROUP_SPANS * GROUP_SPANS
    source = (base + span_source).astype(jnp.int32)
    ordered = frames.reshape(SPANS, SPAN, AUDIO)[source].reshape(TOKENS, AUDIO)
    tokens_in = (jnp.dot(ordered, adapter_weight, preferred_element_type=jnp.float32) + adapter_bias).astype(jnp.bfloat16)
    wide = tokens_in.astype(jnp.float32)
    normed = (wide * lax.rsqrt(lax.optimization_barrier(jnp.mean(wide * wide, axis=-1, keepdims=True)) + 1e-06) * norm_gain).astype(jnp.bfloat16)
    projected = jnp.dot(normed, qkv_weight.reshape(D, 3 * D), preferred_element_type=jnp.float32).reshape(TOKENS, 3, HEADS, HEAD)
    positions = (lengths[:, None] + jnp.arange(NEW, dtype=jnp.int32)[None, :]).reshape(TOKENS)
    queries = rotate(projected[:, 0], positions).astype(jnp.bfloat16)
    new_keys = rotate(projected[:, 1], positions).astype(jnp.bfloat16)
    new_values = projected[:, 2].astype(jnp.bfloat16)
    attended = lax.map(attend_one, (queries.reshape(MEETINGS, NEW, HEADS, HEAD), k_cache.reshape(MEETINGS, HIST, HEADS, HEAD), v_cache.reshape(MEETINGS, HIST, HEADS, HEAD), new_keys.reshape(MEETINGS, NEW, HEADS, HEAD), new_values.reshape(MEETINGS, NEW, HEADS, HEAD), lengths))
    attn_out = jnp.dot(attended.reshape(TOKENS, D), out_weight, preferred_element_type=jnp.float32).astype(jnp.bfloat16)
    return (attn_out, new_keys.reshape(TOKENS, D), new_values.reshape(TOKENS, D))
```

```python
import functools

import jax
import jax.numpy as jnp
from jax import lax
from jax.experimental import pallas as pl
from jax.experimental.pallas import tpu as pltpu
from jax.sharding import PartitionSpec as P

HEAD = 128
FLOOR_SCORE = -1e30
MESH = pl.DeviceIdType.MESH
LOW = 2


def layer_kernel(
    nc, nw, meets, hist,
    frames_ref, adapter_ref, bias_ref, gain_ref, cos_ref, sin_ref, live_ref,
    qkv_hbm, ow_hbm, k_hbm, v_hbm,
    out_ref, key_ref, value_ref,
    feat, xin, query_all, qkv_w, k_mem, v_mem, ow_all,
    proj_own, proj_send, pair_in, cross_send, cross_in,
    num_own, num_send, num_in, num_cross_send, num_cross_in,
    stat_own, stat_send, stat_in, stat_cross_send, stat_cross_in,
    sum_own, sum_send, sum_in, sum_cross_send, sum_cross_in,
    new_num, new_stat, attended,
    local_sem,
    fz_s, fz_r, fy_s, fy_r, fx_s, fx_r,
    pair_s, pair_r, cross_s, cross_r,
    qz_s, qz_r, qy_s, qy_r,
    ow_s, ow_r, owf_s, owf_r,
    ny_s, ny_r, nz_s, nz_r, ty_s, ty_r, tz_s, tz_r,
    by_s, by_r, bz_s, bz_r,
):
    nz, nx, ratio = nc // LOW, nw // 2, nc // nw
    rows, cols = key_ref.shape
    heads = cols // HEAD
    new = rows // meets
    c, w = lax.axis_index("ctx"), lax.axis_index("wt")
    z, y = lax.div(c, LOW), lax.rem(c, LOW)
    x, k = lax.div(w, 2), lax.rem(w, 2)
    other_y, other_k = 1 - y, 1 - k
    sibling_c = z * LOW + other_y
    sibling_w = x * 2 + other_k
    scale = HEAD ** (-0.5)
    pending = []

    def up(value, step, size):
        return lax.rem(value + step, size)

    def down(value, step, size):
        return lax.rem(value + size - step, size)

    def remote(src, dst, send, recv, to_c, to_w):
        return pltpu.make_async_remote_copy(
            src_ref=src, dst_ref=dst, send_sem=send, recv_sem=recv,
            device_id=(to_c, to_w), device_id_type=MESH,
        )

    def send(*parts):
        copy = remote(*parts)
        copy.start()
        pending.append(copy)

    def arrived(dst, send_sem, recv_sem):
        remote(dst, dst, send_sem, recv_sem, sibling_c, w).wait_recv()

    loads = [
        pltpu.make_async_copy(qkv_hbm, qkv_w, local_sem.at[0]),
        pltpu.make_async_copy(k_hbm, k_mem, local_sem.at[1]),
        pltpu.make_async_copy(v_hbm, v_mem, local_sem.at[2]),
        pltpu.make_async_copy(ow_hbm, ow_all.at[w], local_sem.at[3]),
    ]
    for load in loads:
        load.start()

    barrier = pltpu.get_barrier_semaphore()
    for step in range(1, nz):
        pl.semaphore_signal(
            barrier, inc=1, device_id=(up(z, step, nz) * LOW + y, w), device_id_type=MESH
        )
    pl.semaphore_signal(barrier, inc=1, device_id=(sibling_c, w), device_id_type=MESH)
    for step in range(1, nw):
        pl.semaphore_signal(barrier, inc=1, device_id=(c, up(w, step, nw)), device_id_type=MESH)
    adapted = jnp.dot(frames_ref[...], adapter_ref[...], preferred_element_type=jnp.float32)
    feat[c] = (adapted + bias_ref[...]).astype(jnp.bfloat16)
    pl.semaphore_wait(barrier, nz - 1 + 1 + nw - 1)

    def spread_z(buffer, s_sem, r_sem):
        for step in range(nz - 1, 0, -1):
            send(
                buffer.at[c], buffer.at[c], s_sem.at[step], r_sem.at[step],
                up(z, step, nz) * LOW + y, w,
            )

    def spread_y(buffer, block, step, s_sem, r_sem):
        send(buffer.at[block], buffer.at[block], s_sem.at[step], r_sem.at[step], sibling_c, w)

    def forward_copy(block):
        target = lax.div(block, ratio)
        slot = w * ratio + lax.rem(block, ratio)
        return target, slot, remote(
            feat.at[block], xin.at[slot], fx_s.at[block], fx_r.at[slot], c, target
        )

    def forward(block):
        target, slot, copy = forward_copy(block)

        @pl.when(target != w)
        def _():
            copy.start()

        @pl.when(target == w)
        def _():
            xin[slot] = feat[block]

    def z_block(step):
        return down(z, step, nz) * LOW + y

    def y_block(step):
        return down(z, step, nz) * LOW + other_y

    spread_y(feat, c, 0, fy_s, fy_r)
    spread_z(feat, fz_s, fz_r)
    forward(c)
    for step in range(nz):
        if step:
            arrived(feat.at[z_block(step)], fz_s.at[step], fz_r.at[step])
            spread_y(feat, z_block(step), step, fy_s, fy_r)
            forward(z_block(step))
        if step:
            arrived(feat.at[y_block(step - 1)], fy_s.at[step - 1], fy_r.at[step - 1])
            forward(y_block(step - 1))
    arrived(feat.at[y_block(nz - 1)], fy_s.at[nz - 1], fy_r.at[nz - 1])
    forward(y_block(nz - 1))

    loads[0].wait()

    def project(group):
        @pl.when(group != w)
        def _():
            for j in range(ratio):
                slot = group * ratio + j
                arrived(xin.at[slot], fx_s.at[j], fx_r.at[slot])

        scaled = [
            (xin[group * ratio + j].astype(jnp.float32) * gain_ref[w * ratio + j]).astype(
                jnp.bfloat16
            )
            for j in range(ratio)
        ]
        lhs = jnp.concatenate(scaled, axis=1)
        return [
            jnp.dot(lhs, qkv_w[kind], preferred_element_type=jnp.float32) for kind in range(3)
        ]

    @pl.loop(0, nx)
    def _(index):
        at = lax.rem(x + 1 + index, nx)
        terms = project(at * 2 + other_k)
        for kind in range(3):
            proj_send[at, kind] = terms[kind].astype(jnp.bfloat16)
        remote(
            proj_send.at[at], pair_in.at[at], pair_s.at[at], pair_r.at[at], c, sibling_w
        ).start()

    @pl.loop(0, nx)
    def _(index):
        at = lax.rem(x + 1 + index, nx)
        terms = project(at * 2 + k)
        for kind in range(3):
            proj_own[at, kind] = terms[kind]

    for step in range(1, nx):
        at = up(x, step, nx)
        arrived(pair_in.at[at], pair_s.at[at], pair_r.at[at])
        for kind in range(3):
            cross_send[step, kind] = (
                proj_own[at, kind] + pair_in[at, kind].astype(jnp.float32)
            ).astype(jnp.bfloat16)
        send(
            cross_send.at[step], cross_in.at[step], cross_s.at[step], cross_r.at[step],
            c, at * 2 + k,
        )

    squares = jnp.zeros((rows, 1), jnp.float32)
    for block in range(nc):
        wide = feat[block].astype(jnp.float32)
        squares += jnp.sum(wide * wide, axis=-1, keepdims=True)
    inverse = lax.rsqrt(squares / (nc * cols) + 1e-06)

    arrived(pair_in.at[x], pair_s.at[x], pair_r.at[x])
    for step in range(1, nx):
        arrived(cross_in.at[step], cross_s.at[step], cross_r.at[step])

    def projected(kind):
        total = proj_own[x, kind] + pair_in[x, kind].astype(jnp.float32)
        for step in range(1, nx):
            total += cross_in[step, kind].astype(jnp.float32)
        return total * inverse

    def rotated(values):
        pieces = []
        for head in range(heads):
            piece = values[:, head * HEAD : (head + 1) * HEAD]
            pieces.append(piece * cos_ref[...] + pltpu.roll(piece, HEAD // 2, 1) * sin_ref[...])
        return jnp.concatenate(pieces, axis=1).astype(jnp.bfloat16)

    query_all[c] = rotated(projected(0))
    spread_y(query_all, c, 0, qy_s, qy_r)
    spread_z(query_all, qz_s, qz_r)
    key_ref[...] = rotated(projected(1))
    value_ref[...] = projected(2).astype(jnp.bfloat16)

    loads[3].wait()
    send(ow_all.at[w], ow_all.at[w], ow_s.at[0], ow_r.at[0], c, sibling_w)
    for step in range(1, nx):
        send(
            ow_all.at[w], ow_all.at[w], ow_s.at[step], ow_r.at[step],
            c, up(x, step, nx) * 2 + k,
        )

    lanes = lax.broadcasted_iota(jnp.int32, (rows, HEAD), 1)

    def attend(query, keys, values, mask, meeting_mask):
        stat = jnp.zeros((rows, HEAD), jnp.float32)
        numers = []
        for head in range(heads):
            at = slice(head * HEAD, (head + 1) * HEAD)
            tops, totals, parts = [], [], []
            for m in range(meets):
                score = lax.dot_general(
                    query[m * new : (m + 1) * new, at], keys[m][:, at],
                    (((1,), (1,)), ((), ())), preferred_element_type=jnp.float32,
                ) * scale
                keep = mask[m] if meeting_mask else mask
                top = jnp.maximum(
                    jnp.max(jnp.where(keep, score, -jnp.inf), axis=-1, keepdims=True), FLOOR_SCORE
                )
                weight = jnp.where(keep, jnp.exp(score - top), 0.0)
                tops.append(top)
                totals.append(jnp.sum(weight, axis=-1, keepdims=True))
                parts.append(
                    jnp.dot(
                        weight.astype(jnp.bfloat16), values[m][:, at],
                        preferred_element_type=jnp.float32,
                    )
                )
            stat = jnp.where(lanes == head, jnp.concatenate(tops, axis=0), stat)
            stat = jnp.where(lanes == heads + head, jnp.concatenate(totals, axis=0), stat)
            numers.append(jnp.concatenate(parts, axis=0))
        return jnp.concatenate(numers, axis=1), stat

    causal = lax.broadcasted_iota(jnp.int32, (new, new), 0) >= lax.broadcasted_iota(
        jnp.int32, (new, new), 1
    )
    new_keys, new_values = key_ref[...], value_ref[...]
    numer, stat = attend(
        query_all[c],
        [new_keys[m * new : (m + 1) * new] for m in range(meets)],
        [new_values[m * new : (m + 1) * new] for m in range(meets)],
        causal, False,
    )
    new_num[...] = numer
    new_stat[...] = stat

    loads[1].wait()
    loads[2].wait()

    def history(block):
        at = pl.ds(pl.multiple_of(block * cols, cols), cols)
        return attend(
            query_all[block],
            [k_mem[m, :, at] for m in range(meets)],
            [v_mem[m, :, at] for m in range(meets)],
            [jnp.broadcast_to(live_ref[m] > 0.5, (new, hist)) for m in range(meets)], True,
        )

    def packed(stat):
        return jnp.transpose(stat)[: stat_send.shape[1]]

    def unpacked(short):
        filled = jnp.concatenate(
            [short, jnp.zeros((HEAD - short.shape[0], rows), jnp.float32)], axis=0
        )
        return jnp.transpose(filled)

    def merge(left, right):
        left_num, left_stat = left
        right_num, right_stat = right
        joint = jnp.maximum(left_stat, right_stat)
        left_scale = jnp.exp(left_stat - joint)
        right_scale = jnp.exp(right_stat - joint)
        stat = jnp.where(lanes < heads, joint, 0.0)
        pieces = []
        for head in range(heads):
            at = slice(head * HEAD, (head + 1) * HEAD)
            one, two = left_scale[:, head : head + 1], right_scale[:, head : head + 1]
            pieces.append(left_num[:, at] * one + right_num[:, at] * two)
            total = (
                left_stat[:, heads + head : heads + head + 1] * one
                + right_stat[:, heads + head : heads + head + 1] * two
            )
            stat = jnp.where(lanes == heads + head, total, stat)
        return jnp.concatenate(pieces, axis=1), stat

    for step in range(1, nz):
        arrived(query_all.at[z_block(step)], qz_s.at[step], qz_r.at[step])
        spread_y(query_all, z_block(step), step, qy_s, qy_r)

    @pl.loop(0, nz)
    def _(step):
        block = y_block(step)
        arrived(query_all.at[block], qy_s.at[step], qy_r.at[step])
        numer, stat = history(block)
        num_send[step] = numer.astype(jnp.bfloat16)
        stat_send[step] = packed(stat)
        remote(
            num_send.at[step], num_in.at[step], ny_s.at[step], ny_r.at[step], sibling_c, w
        ).start()
        remote(
            stat_send.at[step], stat_in.at[step], ty_s.at[step], ty_r.at[step], sibling_c, w
        ).start()

    @pl.loop(0, nz)
    def _(index):
        step = lax.rem(index + 1, nz)
        block = z_block(step)
        own = history(block)
        arrived(num_in.at[step], ny_s.at[step], ny_r.at[step])
        arrived(stat_in.at[step], ty_s.at[step], ty_r.at[step])
        numer, stat = merge(
            own, (num_in[step].astype(jnp.float32), unpacked(stat_in[step]))
        )

        @pl.when(step > 0)
        def _():
            num_cross_send[step] = numer.astype(jnp.bfloat16)
            stat_cross_send[step] = packed(stat)
            remote(
                num_cross_send.at[step], num_cross_in.at[step], nz_s.at[step], nz_r.at[step],
                block, w,
            ).start()
            remote(
                stat_cross_send.at[step], stat_cross_in.at[step], tz_s.at[step], tz_r.at[step],
                block, w,
            ).start()

        @pl.when(step == 0)
        def _():
            numer_all, stat_all = merge((numer, stat), (new_num[...], new_stat[...]))
            num_own[...] = numer_all
            stat_own[...] = stat_all

    for step in range(1, nx):
        origin = down(x, step, nx) * 2 + k
        arrived(ow_all.at[origin], ow_s.at[step], ow_r.at[step])
        send(
            ow_all.at[origin], ow_all.at[origin], owf_s.at[step], owf_r.at[step], c, sibling_w
        )

    for step in range(1, nz):
        arrived(num_cross_in.at[step], nz_s.at[step], nz_r.at[step])
        arrived(stat_cross_in.at[step], tz_s.at[step], tz_r.at[step])
        numer, stat = merge(
            (num_own[...], stat_own[...]),
            (num_cross_in[step].astype(jnp.float32), unpacked(stat_cross_in[step])),
        )
        num_own[...] = numer
        stat_own[...] = stat
    stat = stat_own[...]
    for head in range(heads):
        at = slice(head * HEAD, (head + 1) * HEAD)
        attended[:, at] = (
            num_own[:, at] / stat[:, heads + head : heads + head + 1]
        ).astype(jnp.bfloat16)

    arrived(ow_all.at[sibling_w], ow_s.at[0], ow_r.at[0])
    for step in range(1, nx):
        origin = down(x, step, nx) * 2 + other_k
        arrived(ow_all.at[origin], owf_s.at[step], owf_r.at[step])

    def out_term(block):
        at = pl.ds(pl.multiple_of(lax.rem(block, ratio) * cols, cols), cols)
        return jnp.dot(
            attended[...], ow_all[lax.div(block, ratio), :, at],
            preferred_element_type=jnp.float32,
        )

    @pl.loop(0, nz)
    def _(index):
        step = lax.rem(index + 1, nz)
        sum_send[step] = out_term(y_block(step)).astype(jnp.bfloat16)
        remote(
            sum_send.at[step], sum_in.at[step], by_s.at[step], by_r.at[step], sibling_c, w
        ).start()

    @pl.loop(0, nz)
    def _(index):
        step = lax.rem(index + 1, nz)
        block = z_block(step)
        term = out_term(block)
        arrived(sum_in.at[step], by_s.at[step], by_r.at[step])
        term += sum_in[step].astype(jnp.float32)

        @pl.when(step > 0)
        def _():
            sum_cross_send[step] = term.astype(jnp.bfloat16)
            remote(
                sum_cross_send.at[step], sum_cross_in.at[step], bz_s.at[step], bz_r.at[step],
                block, w,
            ).start()

        @pl.when(step == 0)
        def _():
            sum_own[...] = term

    total = sum_own[...]
    for step in range(1, nz):
        arrived(sum_cross_in.at[step], bz_s.at[step], bz_r.at[step])
        total += sum_cross_in[step].astype(jnp.float32)
    out_ref[...] = total.astype(jnp.bfloat16)

    def left(src, send_sem, recv_sem):
        remote(src, src, send_sem, recv_sem, sibling_c, w).wait_send()

    for copy in pending:
        copy.wait_send()
    for block in range(nc):
        target, _, copy = forward_copy(block)

        @pl.when(target != w)
        def _():
            copy.wait_send()

    for at in range(nx):
        left(proj_send.at[at], pair_s.at[at], pair_r.at[at])
    for step in range(nz):
        left(num_send.at[step], ny_s.at[step], ny_r.at[step])
        left(stat_send.at[step], ty_s.at[step], ty_r.at[step])
        left(sum_send.at[step], by_s.at[step], by_r.at[step])
        if step:
            left(num_cross_send.at[step], nz_s.at[step], nz_r.at[step])
            left(stat_cross_send.at[step], tz_s.at[step], tz_r.at[step])
            left(sum_cross_send.at[step], bz_s.at[step], bz_r.at[step])


def shards(
    nc, nw,
    frames, span_source, adapter_weight, adapter_bias, norm_gain,
    qkv_weight, out_weight, k_cache, v_cache, lengths,
):
    rows, audio_width = frames.shape
    group_spans = span_source.shape[0]
    meets, hist, width = k_cache.shape
    depth, _, cols = qkv_weight.shape
    new = rows // meets
    nz, nx = nc // LOW, nw // 2
    heads = cols // HEAD
    short = max(8, (2 * heads + 7) // 8 * 8)
    ordered = frames.reshape(group_spans, rows // group_spans, audio_width)[span_source].reshape(
        rows, audio_width
    )
    half = HEAD // 2
    positions = (lengths[:, None] + jnp.arange(new, dtype=jnp.int32)[None, :]).reshape(rows)
    freq = 10000.0 ** (-2.0 * jnp.arange(half, dtype=jnp.float32) / HEAD)
    angle = positions.astype(jnp.float32)[:, None] * freq[None, :]
    cosine, sine = jnp.cos(angle), jnp.sin(angle)
    cosines = jnp.concatenate([cosine, cosine], axis=1)
    sines = jnp.concatenate([-sine, sine], axis=1)
    place = lax.axis_index("ctx") * hist + jnp.arange(hist, dtype=jnp.int32)
    live = (place[None, :] < lengths[:, None]).astype(jnp.float32)[:, None, :]
    vmem = pl.BlockSpec(memory_space=pltpu.VMEM)
    anywhere = pl.BlockSpec(memory_space=pl.ANY)
    half_type, full_type = jnp.bfloat16, jnp.float32
    block = (rows, cols)
    dma = lambda count: pltpu.SemaphoreType.DMA((count,))
    result = jax.ShapeDtypeStruct(block, half_type)
    return pl.pallas_call(
        functools.partial(layer_kernel, nc, nw, meets, hist),
        out_shape=(result, result, result),
        in_specs=[vmem] * 7 + [anywhere] * 4,
        out_specs=(vmem, vmem, vmem),
        scratch_shapes=[
            pltpu.VMEM((nc,) + block, half_type),
            pltpu.VMEM((nc,) + block, half_type),
            pltpu.VMEM((nc,) + block, half_type),
            pltpu.VMEM((3, depth, cols), half_type),
            pltpu.VMEM((meets, hist, width), half_type),
            pltpu.VMEM((meets, hist, width), half_type),
            pltpu.VMEM((nw,) + out_weight.shape, half_type),
            pltpu.VMEM((nx, 3) + block, full_type),
            pltpu.VMEM((nx, 3) + block, half_type),
            pltpu.VMEM((nx, 3) + block, half_type),
            pltpu.VMEM((nx, 3) + block, half_type),
            pltpu.VMEM((nx, 3) + block, half_type),
            pltpu.VMEM(block, full_type),
            pltpu.VMEM((nz,) + block, half_type),
            pltpu.VMEM((nz,) + block, half_type),
            pltpu.VMEM((nz,) + block, half_type),
            pltpu.VMEM((nz,) + block, half_type),
            pltpu.VMEM((rows, HEAD), full_type),
            pltpu.VMEM((nz, short, rows), full_type),
            pltpu.VMEM((nz, short, rows), full_type),
            pltpu.VMEM((nz, short, rows), full_type),
            pltpu.VMEM((nz, short, rows), full_type),
            pltpu.VMEM(block, full_type),
            pltpu.VMEM((nz,) + block, half_type),
            pltpu.VMEM((nz,) + block, half_type),
            pltpu.VMEM((nz,) + block, half_type),
            pltpu.VMEM((nz,) + block, half_type),
            pltpu.VMEM(block, full_type),
            pltpu.VMEM((rows, HEAD), full_type),
            pltpu.VMEM(block, half_type),
            dma(4),
            dma(nz), dma(nz), dma(nz), dma(nz), dma(nc), dma(nc),
            dma(nx), dma(nx), dma(nx), dma(nx),
            dma(nz), dma(nz), dma(nz), dma(nz),
            dma(nx), dma(nx), dma(nx), dma(nx),
            dma(nz), dma(nz), dma(nz), dma(nz), dma(nz), dma(nz), dma(nz), dma(nz),
            dma(nz), dma(nz), dma(nz), dma(nz),
        ],
        compiler_params=pltpu.CompilerParams(
            collective_id=0, has_side_effects=True, vmem_limit_bytes=48 * 1024 * 1024
        ),
        cost_estimate=pl.CostEstimate(
            flops=8 * rows * depth * 3 * cols,
            bytes_accessed=2 * (3 * depth * cols + 2 * meets * hist * width),
            transcendentals=0,
        ),
    )(
        ordered, adapter_weight, adapter_bias.reshape(1, cols), norm_gain.reshape(nc, 1, cols),
        cosines, sines, live,
        jnp.transpose(qkv_weight, (1, 0, 2)), out_weight, k_cache, v_cache,
    )


def solution(mesh):
    nc, nw = mesh.shape["ctx"], mesh.shape["wt"]
    return jax.shard_map(
        functools.partial(shards, nc, nw),
        mesh=mesh,
        in_specs=(
            P("wt", None),
            P("wt"),
            P(None, "ctx"),
            P("ctx"),
            P(),
            P("wt", None, "ctx"),
            P("ctx", "wt"),
            P("wt", "ctx", None),
            P("wt", "ctx", None),
            P("wt"),
        ),
        out_specs=(P("wt", "ctx"), P("wt", "ctx"), P("wt", "ctx")),
        check_vma=False,
    )
```

```python
import functools
import math

import jax
import jax.numpy as jnp
from jax import lax
from jax.experimental import pallas as pl
from jax.experimental.pallas import tpu as pltpu
from jax.sharding import PartitionSpec as P

HEAD = 128
FLOOR_SCORE = -1e30
MESH = pl.DeviceIdType.MESH
LOW = 2


def layer_kernel(
    nc, nw, meets, hist,
    source_ref, lengths_ref,
    frames_hbm, adapter_hbm, bias_hbm, gain_hbm, qkv_hbm, ow_hbm, k_hbm, v_hbm,
    out_ref, key_ref, value_ref,
    frames_ref, adapter_ref, bias_ref, gain_ref, cos_ref, sin_ref, lhs,
    feat, xin, query_all, qkv_w, k_mem, v_mem, ow_all,
    proj_own, proj_send, pair_in, cross_send, cross_in,
    num_own, num_send, num_in, num_cross_send, num_cross_in,
    stat_own, stat_send, stat_in, stat_cross_send, stat_cross_in,
    sum_own, sum_send, sum_in, sum_cross_send, sum_cross_in,
    new_num, new_stat, attended,
    local_sem,
    fz_s, fz_r, fy_s, fy_r, fx_s, fx_r,
    pair_s, pair_r, cross_s, cross_r,
    qz_s, qz_r, qy_s, qy_r,
    ow_s, ow_r, owf_s, owf_r,
    ny_s, ny_r, nz_s, nz_r, ty_s, ty_r, tz_s, tz_r,
    by_s, by_r, bz_s, bz_r,
):
    nz, nx, ratio = nc // LOW, nw // 2, nc // nw
    rows, cols = key_ref.shape
    heads = cols // HEAD
    new = rows // meets
    c, w = lax.axis_index("ctx"), lax.axis_index("wt")
    z, y = lax.div(c, LOW), lax.rem(c, LOW)
    x, k = lax.div(w, 2), lax.rem(w, 2)
    other_y, other_k = 1 - y, 1 - k
    sibling_c = z * LOW + other_y
    sibling_w = x * 2 + other_k
    scale = HEAD ** (-0.5)
    pending = []

    def up(value, step, size):
        return lax.rem(value + step, size)

    def down(value, step, size):
        return lax.rem(value + size - step, size)

    def remote(src, dst, send, recv, to_c, to_w):
        return pltpu.make_async_remote_copy(
            src_ref=src, dst_ref=dst, send_sem=send, recv_sem=recv,
            device_id=(to_c, to_w), device_id_type=MESH,
        )

    def send(*parts):
        copy = remote(*parts)
        copy.start()
        pending.append(copy)

    def arrived(dst, send_sem, recv_sem):
        remote(dst, dst, send_sem, recv_sem, sibling_c, w).wait_recv()

    loads = [
        pltpu.make_async_copy(qkv_hbm, qkv_w, local_sem.at[0]),
        pltpu.make_async_copy(k_hbm, k_mem, local_sem.at[1]),
        pltpu.make_async_copy(v_hbm, v_mem, local_sem.at[2]),
        pltpu.make_async_copy(ow_hbm, ow_all.at[w], local_sem.at[3]),
        pltpu.make_async_copy(frames_hbm, frames_ref, local_sem.at[4]),
        pltpu.make_async_copy(adapter_hbm, adapter_ref, local_sem.at[5]),
        pltpu.make_async_copy(bias_hbm, bias_ref, local_sem.at[6]),
        pltpu.make_async_copy(gain_hbm, gain_ref, local_sem.at[7]),
    ]
    for load in loads[4:] + loads[:4]:
        load.start()

    barrier = pltpu.get_barrier_semaphore()
    for step in range(1, nz):
        pl.semaphore_signal(
            barrier, inc=1, device_id=(up(z, step, nz) * LOW + y, w), device_id_type=MESH
        )
    pl.semaphore_signal(barrier, inc=1, device_id=(sibling_c, w), device_id_type=MESH)
    for step in range(1, nw):
        pl.semaphore_signal(barrier, inc=1, device_id=(c, up(w, step, nw)), device_id_type=MESH)
    for load in loads[4:]:
        load.wait()
    spans = frames_ref.shape[0]
    ordered = jnp.concatenate([frames_ref[source_ref[slot]] for slot in range(spans)], axis=0)
    adapted = jnp.dot(ordered, adapter_ref[...], preferred_element_type=jnp.float32)
    feat[c] = (adapted + bias_ref[...]).astype(jnp.bfloat16)
    pl.semaphore_wait(barrier, nz - 1 + 1 + nw - 1)

    def spread_z(buffer, s_sem, r_sem):
        for step in range(nz - 1, 0, -1):
            send(
                buffer.at[c], buffer.at[c], s_sem.at[step], r_sem.at[step],
                up(z, step, nz) * LOW + y, w,
            )

    def spread_y(buffer, block, step, s_sem, r_sem):
        send(buffer.at[block], buffer.at[block], s_sem.at[step], r_sem.at[step], sibling_c, w)

    def forward_copy(block):
        target = lax.div(block, ratio)
        slot = w * ratio + lax.rem(block, ratio)
        return target, slot, remote(
            feat.at[block], xin.at[slot], fx_s.at[block], fx_r.at[slot], c, target
        )

    def forward(block):
        target, slot, copy = forward_copy(block)

        @pl.when(target != w)
        def _():
            copy.start()

        @pl.when(target == w)
        def _():
            xin[slot] = feat[block]

    def z_block(step):
        return down(z, step, nz) * LOW + y

    def y_block(step):
        return down(z, step, nz) * LOW + other_y

    lanes = lax.broadcasted_iota(jnp.int32, (rows, HEAD), 1)
    tokens = lax.broadcasted_iota(jnp.int32, (rows, HEAD), 0)

    spread_y(feat, c, 0, fy_s, fy_r)
    spread_z(feat, fz_s, fz_r)
    forward(c)

    place = tokens + lengths_ref[0]
    for m in range(1, meets):
        place = jnp.where(tokens >= m * new, tokens - m * new + lengths_ref[m], place)
    twice = jnp.where(lanes < HEAD // 2, lanes, lanes - HEAD // 2).astype(jnp.float32)
    angle = place.astype(jnp.float32) * jnp.exp(twice * (-2.0 / HEAD * math.log(10000.0)))
    cos_ref[...] = jnp.cos(angle)
    sin_ref[...] = jnp.sin(angle) * jnp.where(lanes < HEAD // 2, -1.0, 1.0)

    for step in range(nz):
        if step:
            arrived(feat.at[z_block(step)], fz_s.at[step], fz_r.at[step])
            spread_y(feat, z_block(step), step, fy_s, fy_r)
            forward(z_block(step))
        if step:
            arrived(feat.at[y_block(step - 1)], fy_s.at[step - 1], fy_r.at[step - 1])
            forward(y_block(step - 1))
    arrived(feat.at[y_block(nz - 1)], fy_s.at[nz - 1], fy_r.at[nz - 1])
    forward(y_block(nz - 1))

    loads[0].wait()

    def gather_rows(side, core):
        for index in range(nx):
            group = index * 2 + core

            @pl.when(group != w)
            def _():
                for j in range(ratio):
                    slot = group * ratio + j
                    arrived(xin.at[slot], fx_s.at[j], fx_r.at[slot])

            for j in range(ratio):
                lhs[side, pl.ds(index * rows, rows), pl.ds(j * cols, cols)] = (
                    xin[group * ratio + j].astype(jnp.float32) * gain_ref[w * ratio + j]
                ).astype(jnp.bfloat16)

    def project(side, kind):
        total = jnp.dot(lhs[side], qkv_w[kind], preferred_element_type=jnp.float32)
        return [total[at * rows : (at + 1) * rows] for at in range(nx)]

    def project_pair(kind):
        for at, term in enumerate(project(1, kind)):
            proj_send[at, kind] = term.astype(jnp.bfloat16)
            send(
                proj_send.at[at, kind], pair_in.at[at, kind],
                pair_s.at[at * 3 + kind], pair_r.at[at * 3 + kind], c, sibling_w,
            )

    def project_own(kind):
        for at, term in enumerate(project(0, kind)):
            proj_own[at, kind] = term

    def pass_on(kind):
        for at in range(nx):
            arrived(
                pair_in.at[at, kind], pair_s.at[at * 3 + kind], pair_r.at[at * 3 + kind]
            )
        for step in range(1, nx):
            at = up(x, step, nx)
            cross_send[step, kind] = (
                proj_own[at, kind] + pair_in[at, kind].astype(jnp.float32)
            ).astype(jnp.bfloat16)
            send(
                cross_send.at[step, kind], cross_in.at[step, kind],
                cross_s.at[step * 3 + kind], cross_r.at[step * 3 + kind], c, at * 2 + k,
            )

    gather_rows(1, other_k)
    project_pair(0)
    gather_rows(0, k)
    project_own(0)
    pass_on(0)
    project_pair(1)
    project_pair(2)

    squares = jnp.zeros((rows, 1), jnp.float32)
    for block in range(nc):
        wide = feat[block].astype(jnp.float32)
        squares += jnp.sum(wide * wide, axis=-1, keepdims=True)
    inverse = lax.rsqrt(squares / (nc * cols) + 1e-06)

    def projected(kind):
        total = proj_own[x, kind] + pair_in[x, kind].astype(jnp.float32)
        for step in range(1, nx):
            arrived(
                cross_in.at[step, kind], cross_s.at[step * 3 + kind], cross_r.at[step * 3 + kind]
            )
            total += cross_in[step, kind].astype(jnp.float32)
        return total * inverse

    def rotated(values):
        pieces = []
        for head in range(heads):
            piece = values[:, head * HEAD : (head + 1) * HEAD]
            pieces.append(piece * cos_ref[...] + pltpu.roll(piece, HEAD // 2, 1) * sin_ref[...])
        return jnp.concatenate(pieces, axis=1).astype(jnp.bfloat16)

    query_all[c] = rotated(projected(0))
    spread_y(query_all, c, 0, qy_s, qy_r)
    spread_z(query_all, qz_s, qz_r)
    for kind in (1, 2):
        project_own(kind)
        pass_on(kind)

    loads[3].wait()
    send(ow_all.at[w], ow_all.at[w], ow_s.at[0], ow_r.at[0], c, sibling_w)
    for step in range(1, nx):
        send(
            ow_all.at[w], ow_all.at[w], ow_s.at[step], ow_r.at[step],
            c, up(x, step, nx) * 2 + k,
        )

    for step in range(1, nz):
        arrived(query_all.at[z_block(step)], qz_s.at[step], qz_r.at[step])
        spread_y(query_all, z_block(step), step, qy_s, qy_r)
    key_ref[...] = rotated(projected(1))
    value_ref[...] = projected(2).astype(jnp.bfloat16)

    def attend(query, keys, values, mask, meeting_mask):
        stat = jnp.zeros((rows, HEAD), jnp.float32)
        numers = []
        for head in range(heads):
            at = slice(head * HEAD, (head + 1) * HEAD)
            tops, totals, parts = [], [], []
            for m in range(meets):
                score = lax.dot_general(
                    query[m * new : (m + 1) * new, at], keys[m][:, at],
                    (((1,), (1,)), ((), ())), preferred_element_type=jnp.float32,
                ) * scale
                keep = mask[m] if meeting_mask else mask
                top = jnp.maximum(
                    jnp.max(jnp.where(keep, score, -jnp.inf), axis=-1, keepdims=True), FLOOR_SCORE
                )
                weight = jnp.where(keep, jnp.exp(score - top), 0.0)
                tops.append(top)
                totals.append(jnp.sum(weight, axis=-1, keepdims=True))
                parts.append(
                    jnp.dot(
                        weight.astype(jnp.bfloat16), values[m][:, at],
                        preferred_element_type=jnp.float32,
                    )
                )
            stat = jnp.where(lanes == head, jnp.concatenate(tops, axis=0), stat)
            stat = jnp.where(lanes == heads + head, jnp.concatenate(totals, axis=0), stat)
            numers.append(jnp.concatenate(parts, axis=0))
        return jnp.concatenate(numers, axis=1), stat

    causal = lax.broadcasted_iota(jnp.int32, (new, new), 0) >= lax.broadcasted_iota(
        jnp.int32, (new, new), 1
    )
    new_keys, new_values = key_ref[...], value_ref[...]
    numer, stat = attend(
        query_all[c],
        [new_keys[m * new : (m + 1) * new] for m in range(meets)],
        [new_values[m * new : (m + 1) * new] for m in range(meets)],
        causal, False,
    )
    new_num[...] = numer
    new_stat[...] = stat

    loads[1].wait()
    loads[2].wait()

    cached = c * hist + lax.broadcasted_iota(jnp.int32, (new, hist), 1)

    def history(block):
        at = pl.ds(pl.multiple_of(block * cols, cols), cols)
        return attend(
            query_all[block],
            [k_mem[m, :, at] for m in range(meets)],
            [v_mem[m, :, at] for m in range(meets)],
            [cached < lengths_ref[m] for m in range(meets)], True,
        )

    def packed(stat):
        return jnp.transpose(stat)[: stat_send.shape[1]]

    def unpacked(short):
        filled = jnp.concatenate(
            [short, jnp.zeros((HEAD - short.shape[0], rows), jnp.float32)], axis=0
        )
        return jnp.transpose(filled)

    def merge(left, right):
        left_num, left_stat = left
        right_num, right_stat = right
        joint = jnp.maximum(left_stat, right_stat)
        left_scale = jnp.exp(left_stat - joint)
        right_scale = jnp.exp(right_stat - joint)
        stat = jnp.where(lanes < heads, joint, 0.0)
        pieces = []
        for head in range(heads):
            at = slice(head * HEAD, (head + 1) * HEAD)
            one, two = left_scale[:, head : head + 1], right_scale[:, head : head + 1]
            pieces.append(left_num[:, at] * one + right_num[:, at] * two)
            total = (
                left_stat[:, heads + head : heads + head + 1] * one
                + right_stat[:, heads + head : heads + head + 1] * two
            )
            stat = jnp.where(lanes == heads + head, total, stat)
        return jnp.concatenate(pieces, axis=1), stat

    @pl.loop(0, nz)
    def _(step):
        block = y_block(step)
        arrived(query_all.at[block], qy_s.at[step], qy_r.at[step])
        numer, stat = history(block)
        num_send[step] = numer.astype(jnp.bfloat16)
        stat_send[step] = packed(stat)
        remote(
            num_send.at[step], num_in.at[step], ny_s.at[step], ny_r.at[step], sibling_c, w
        ).start()
        remote(
            stat_send.at[step], stat_in.at[step], ty_s.at[step], ty_r.at[step], sibling_c, w
        ).start()

    @pl.loop(0, nz)
    def _(index):
        step = lax.rem(index + 1, nz)
        block = z_block(step)
        own = history(block)
        arrived(num_in.at[step], ny_s.at[step], ny_r.at[step])
        arrived(stat_in.at[step], ty_s.at[step], ty_r.at[step])
        numer, stat = merge(
            own, (num_in[step].astype(jnp.float32), unpacked(stat_in[step]))
        )

        @pl.when(step > 0)
        def _():
            num_cross_send[step] = numer.astype(jnp.bfloat16)
            stat_cross_send[step] = packed(stat)
            remote(
                num_cross_send.at[step], num_cross_in.at[step], nz_s.at[step], nz_r.at[step],
                block, w,
            ).start()
            remote(
                stat_cross_send.at[step], stat_cross_in.at[step], tz_s.at[step], tz_r.at[step],
                block, w,
            ).start()

        @pl.when(step == 0)
        def _():
            numer_all, stat_all = merge((numer, stat), (new_num[...], new_stat[...]))
            num_own[...] = numer_all
            stat_own[...] = stat_all

    for step in range(1, nx):
        origin = down(x, step, nx) * 2 + k
        arrived(ow_all.at[origin], ow_s.at[step], ow_r.at[step])
        send(
            ow_all.at[origin], ow_all.at[origin], owf_s.at[step], owf_r.at[step], c, sibling_w
        )

    for step in range(1, nz):
        arrived(num_cross_in.at[step], nz_s.at[step], nz_r.at[step])
        arrived(stat_cross_in.at[step], tz_s.at[step], tz_r.at[step])
        numer, stat = merge(
            (num_own[...], stat_own[...]),
            (num_cross_in[step].astype(jnp.float32), unpacked(stat_cross_in[step])),
        )
        num_own[...] = numer
        stat_own[...] = stat
    stat = stat_own[...]
    for head in range(heads):
        at = slice(head * HEAD, (head + 1) * HEAD)
        attended[:, at] = (
            num_own[:, at] / stat[:, heads + head : heads + head + 1]
        ).astype(jnp.bfloat16)

    arrived(ow_all.at[sibling_w], ow_s.at[0], ow_r.at[0])
    for step in range(1, nx):
        origin = down(x, step, nx) * 2 + other_k
        arrived(ow_all.at[origin], owf_s.at[step], owf_r.at[step])

    def out_term(block):
        at = pl.ds(pl.multiple_of(lax.rem(block, ratio) * cols, cols), cols)
        return jnp.dot(
            attended[...], ow_all[lax.div(block, ratio), :, at],
            preferred_element_type=jnp.float32,
        )

    @pl.loop(0, nz)
    def _(index):
        step = lax.rem(index + 1, nz)
        sum_send[step] = out_term(y_block(step)).astype(jnp.bfloat16)
        remote(
            sum_send.at[step], sum_in.at[step], by_s.at[step], by_r.at[step], sibling_c, w
        ).start()

    @pl.loop(0, nz)
    def _(index):
        step = lax.rem(index + 1, nz)
        block = z_block(step)
        term = out_term(block)
        arrived(sum_in.at[step], by_s.at[step], by_r.at[step])
        term += sum_in[step].astype(jnp.float32)

        @pl.when(step > 0)
        def _():
            sum_cross_send[step] = term.astype(jnp.bfloat16)
            remote(
                sum_cross_send.at[step], sum_cross_in.at[step], bz_s.at[step], bz_r.at[step],
                block, w,
            ).start()

        @pl.when(step == 0)
        def _():
            sum_own[...] = term

    total = sum_own[...]
    for step in range(1, nz):
        arrived(sum_cross_in.at[step], bz_s.at[step], bz_r.at[step])
        total += sum_cross_in[step].astype(jnp.float32)
    out_ref[...] = total.astype(jnp.bfloat16)

    def left(src, send_sem, recv_sem):
        remote(src, src, send_sem, recv_sem, sibling_c, w).wait_send()

    for copy in pending:
        copy.wait_send()
    for block in range(nc):
        target, _, copy = forward_copy(block)

        @pl.when(target != w)
        def _():
            copy.wait_send()

    for step in range(nz):
        left(num_send.at[step], ny_s.at[step], ny_r.at[step])
        left(stat_send.at[step], ty_s.at[step], ty_r.at[step])
        left(sum_send.at[step], by_s.at[step], by_r.at[step])
        if step:
            left(num_cross_send.at[step], nz_s.at[step], nz_r.at[step])
            left(stat_cross_send.at[step], tz_s.at[step], tz_r.at[step])
            left(sum_cross_send.at[step], bz_s.at[step], bz_r.at[step])


def shards(
    nc, nw,
    frames, span_source, adapter_weight, adapter_bias, norm_gain,
    qkv_weight, out_weight, k_cache, v_cache, lengths,
):
    rows, audio_width = frames.shape
    group_spans = span_source.shape[0]
    meets, hist, width = k_cache.shape
    depth, _, cols = qkv_weight.shape
    nz, nx = nc // LOW, nw // 2
    heads = cols // HEAD
    short = max(8, (2 * heads + 7) // 8 * 8)
    vmem = pl.BlockSpec(memory_space=pltpu.VMEM)
    smem = pl.BlockSpec(memory_space=pltpu.SMEM)
    anywhere = pl.BlockSpec(memory_space=pl.ANY)
    half_type, full_type = jnp.bfloat16, jnp.float32
    block = (rows, cols)
    dma = lambda count: pltpu.SemaphoreType.DMA((count,))
    result = jax.ShapeDtypeStruct(block, half_type)
    return pl.pallas_call(
        functools.partial(layer_kernel, nc, nw, meets, hist),
        out_shape=(result, result, result),
        in_specs=[smem] * 2 + [anywhere] * 8,
        out_specs=(vmem, vmem, vmem),
        scratch_shapes=[
            pltpu.VMEM((group_spans, rows // group_spans, audio_width), half_type),
            pltpu.VMEM((audio_width, cols), half_type),
            pltpu.VMEM((1, cols), full_type),
            pltpu.VMEM((nc, 1, cols), full_type),
            pltpu.VMEM((rows, HEAD), full_type),
            pltpu.VMEM((rows, HEAD), full_type),
            pltpu.VMEM((2, nx * rows, depth), half_type),
            pltpu.VMEM((nc,) + block, half_type),
            pltpu.VMEM((nc,) + block, half_type),
            pltpu.VMEM((nc,) + block, half_type),
            pltpu.VMEM((3, depth, cols), half_type),
            pltpu.VMEM((meets, hist, width), half_type),
            pltpu.VMEM((meets, hist, width), half_type),
            pltpu.VMEM((nw,) + out_weight.shape, half_type),
            pltpu.VMEM((nx, 3) + block, full_type),
            pltpu.VMEM((nx, 3) + block, half_type),
            pltpu.VMEM((nx, 3) + block, half_type),
            pltpu.VMEM((nx, 3) + block, half_type),
            pltpu.VMEM((nx, 3) + block, half_type),
            pltpu.VMEM(block, full_type),
            pltpu.VMEM((nz,) + block, half_type),
            pltpu.VMEM((nz,) + block, half_type),
            pltpu.VMEM((nz,) + block, half_type),
            pltpu.VMEM((nz,) + block, half_type),
            pltpu.VMEM((rows, HEAD), full_type),
            pltpu.VMEM((nz, short, rows), full_type),
            pltpu.VMEM((nz, short, rows), full_type),
            pltpu.VMEM((nz, short, rows), full_type),
            pltpu.VMEM((nz, short, rows), full_type),
            pltpu.VMEM(block, full_type),
            pltpu.VMEM((nz,) + block, half_type),
            pltpu.VMEM((nz,) + block, half_type),
            pltpu.VMEM((nz,) + block, half_type),
            pltpu.VMEM((nz,) + block, half_type),
            pltpu.VMEM(block, full_type),
            pltpu.VMEM((rows, HEAD), full_type),
            pltpu.VMEM(block, half_type),
            dma(8),
            dma(nz), dma(nz), dma(nz), dma(nz), dma(nc), dma(nc),
            dma(3 * nx), dma(3 * nx), dma(3 * nx), dma(3 * nx),
            dma(nz), dma(nz), dma(nz), dma(nz),
            dma(nx), dma(nx), dma(nx), dma(nx),
            dma(nz), dma(nz), dma(nz), dma(nz), dma(nz), dma(nz), dma(nz), dma(nz),
            dma(nz), dma(nz), dma(nz), dma(nz),
        ],
        compiler_params=pltpu.CompilerParams(
            collective_id=0, has_side_effects=True, vmem_limit_bytes=60 * 1024 * 1024
        ),
        cost_estimate=pl.CostEstimate(
            flops=8 * rows * depth * 3 * cols,
            bytes_accessed=2 * (3 * depth * cols + 2 * meets * hist * width),
            transcendentals=0,
        ),
    )(
        span_source, lengths,
        frames.reshape(group_spans, rows // group_spans, audio_width), adapter_weight,
        adapter_bias.reshape(1, cols), norm_gain.reshape(nc, 1, cols),
        jnp.transpose(qkv_weight, (1, 0, 2)), out_weight, k_cache, v_cache,
    )


def solution(mesh):
    nc, nw = mesh.shape["ctx"], mesh.shape["wt"]
    return jax.shard_map(
        functools.partial(shards, nc, nw),
        mesh=mesh,
        in_specs=(
            P("wt", None),
            P("wt"),
            P(None, "ctx"),
            P("ctx"),
            P(),
            P("wt", None, "ctx"),
            P("ctx", "wt"),
            P("wt", "ctx", None),
            P("wt", "ctx", None),
            P("wt"),
        ),
        out_specs=(P("wt", "ctx"), P("wt", "ctx"), P("wt", "ctx")),
        check_vma=False,
    )
```

```python
import functools
import math

import jax
import jax.numpy as jnp
from jax import lax
from jax.experimental import pallas as pl
from jax.experimental.pallas import tpu as pltpu
from jax.sharding import PartitionSpec as P

HEAD = 128
FLOOR_SCORE = -1e30
MESH = pl.DeviceIdType.MESH
LOW = 2


def layer_kernel(
    nc, nw, meets, hist,
    source_ref, lengths_ref,
    frames_hbm, adapter_hbm, bias_hbm, gain_hbm, qkv_hbm, ow_hbm, k_hbm, v_hbm,
    out_ref, key_ref, value_ref,
    frames_ref, adapter_ref, bias_ref, gain_ref, cos_ref, sin_ref, lhs,
    feat, xin, query_all, qkv_w, k_mem, v_mem, ow_all,
    proj_own, proj_send, pair_in, cross_send, cross_in,
    num_own, num_send, num_in, num_cross_send, num_cross_in,
    stat_own, stat_send, stat_in, stat_cross_send, stat_cross_in,
    sum_own, sum_send, sum_in, sum_cross_send, sum_cross_in,
    attended,
    local_sem,
    fz_s, fz_r, fy_s, fy_r, fx_s, fx_r,
    pair_s, pair_r, cross_s, cross_r,
    qz_s, qz_r, qy_s, qy_r,
    ow_s, ow_r, owf_s, owf_r,
    ny_s, ny_r, nz_s, nz_r, ty_s, ty_r, tz_s, tz_r,
    by_s, by_r, bz_s, bz_r,
):
    nz, nx, ratio = nc // LOW, nw // 2, nc // nw
    rows, cols = key_ref.shape
    heads = cols // HEAD
    new = rows // meets
    c, w = lax.axis_index("ctx"), lax.axis_index("wt")
    z, y = lax.div(c, LOW), lax.rem(c, LOW)
    x, k = lax.div(w, 2), lax.rem(w, 2)
    other_y, other_k = 1 - y, 1 - k
    sibling_c = z * LOW + other_y
    sibling_w = x * 2 + other_k
    scale = HEAD ** (-0.5)
    pending = []

    def up(value, step, size):
        return lax.rem(value + step, size)

    def down(value, step, size):
        return lax.rem(value + size - step, size)

    def remote(src, dst, send, recv, to_c, to_w):
        return pltpu.make_async_remote_copy(
            src_ref=src, dst_ref=dst, send_sem=send, recv_sem=recv,
            device_id=(to_c, to_w), device_id_type=MESH,
        )

    def send(*parts):
        copy = remote(*parts)
        copy.start()
        pending.append(copy)

    def arrived(dst, send_sem, recv_sem):
        remote(dst, dst, send_sem, recv_sem, sibling_c, w).wait_recv()

    loads = [
        pltpu.make_async_copy(qkv_hbm, qkv_w, local_sem.at[0]),
        pltpu.make_async_copy(k_hbm, k_mem, local_sem.at[1]),
        pltpu.make_async_copy(v_hbm, v_mem, local_sem.at[2]),
        pltpu.make_async_copy(ow_hbm, ow_all.at[w], local_sem.at[3]),
        pltpu.make_async_copy(frames_hbm, frames_ref, local_sem.at[4]),
        pltpu.make_async_copy(adapter_hbm, adapter_ref, local_sem.at[5]),
        pltpu.make_async_copy(bias_hbm, bias_ref, local_sem.at[6]),
        pltpu.make_async_copy(gain_hbm, gain_ref, local_sem.at[7]),
    ]
    for load in loads[4:] + loads[:4]:
        load.start()

    barrier = pltpu.get_barrier_semaphore()
    for step in range(1, nz):
        pl.semaphore_signal(
            barrier, inc=1, device_id=(up(z, step, nz) * LOW + y, w), device_id_type=MESH
        )
    pl.semaphore_signal(barrier, inc=1, device_id=(sibling_c, w), device_id_type=MESH)
    for step in range(1, nw):
        pl.semaphore_signal(barrier, inc=1, device_id=(c, up(w, step, nw)), device_id_type=MESH)
    for load in loads[4:]:
        load.wait()
    spans = frames_ref.shape[0]
    ordered = jnp.concatenate([frames_ref[source_ref[slot]] for slot in range(spans)], axis=0)
    adapted = jnp.dot(ordered, adapter_ref[...], preferred_element_type=jnp.float32)
    feat[c] = (adapted + bias_ref[...]).astype(jnp.bfloat16)
    pl.semaphore_wait(barrier, nz - 1 + 1 + nw - 1)

    def spread_z(buffer, s_sem, r_sem):
        for step in range(nz - 1, 0, -1):
            send(
                buffer.at[c], buffer.at[c], s_sem.at[step], r_sem.at[step],
                up(z, step, nz) * LOW + y, w,
            )

    def spread_y(buffer, block, step, s_sem, r_sem):
        send(buffer.at[block], buffer.at[block], s_sem.at[step], r_sem.at[step], sibling_c, w)

    def forward_copy(block):
        target = lax.div(block, ratio)
        slot = w * ratio + lax.rem(block, ratio)
        return target, slot, remote(
            feat.at[block], xin.at[slot], fx_s.at[block], fx_r.at[slot], c, target
        )

    def forward(block):
        target, slot, copy = forward_copy(block)

        @pl.when(target != w)
        def _():
            copy.start()

        @pl.when(target == w)
        def _():
            xin[slot] = feat[block]

    def z_block(step):
        return down(z, step, nz) * LOW + y

    def y_block(step):
        return down(z, step, nz) * LOW + other_y

    lanes = lax.broadcasted_iota(jnp.int32, (rows, HEAD), 1)
    tokens = lax.broadcasted_iota(jnp.int32, (rows, HEAD), 0)

    first_z, last_z, odd_z = z == 0, z == nz - 1, lax.rem(z, 2)

    def near(index):
        if nz != 4:
            return index
        second = jnp.where(first_z | last_z, 2, 3)
        third = jnp.where(first_z, 1, jnp.where(last_z, 3, 2))
        ranked = jnp.where(index == 1, jnp.where(first_z, 3, 1), jnp.where(index == 2, second, third))
        return jnp.where(index == 0, 0, ranked)

    def far(index):
        if nz != 4:
            return (index + 1) % nz
        return (2, 1 + 2 * odd_z, 3 - 2 * odd_z, 0)[index]

    spread_y(feat, c, 0, fy_s, fy_r)
    spread_z(feat, fz_s, fz_r)
    forward(c)

    place = tokens + lengths_ref[0]
    for m in range(1, meets):
        place = jnp.where(tokens >= m * new, tokens - m * new + lengths_ref[m], place)
    twice = jnp.where(lanes < HEAD // 2, lanes, lanes - HEAD // 2).astype(jnp.float32)
    angle = place.astype(jnp.float32) * jnp.exp(twice * (-2.0 / HEAD * math.log(10000.0)))
    cos_ref[...] = jnp.cos(angle)
    sin_ref[...] = jnp.sin(angle) * jnp.where(lanes < HEAD // 2, -1.0, 1.0)

    def take_y(step):
        arrived(feat.at[y_block(step)], fy_s.at[step], fy_r.at[step])
        forward(y_block(step))

    for index in range(1, nz):
        step = near(index)
        arrived(feat.at[z_block(step)], fz_s.at[step], fz_r.at[step])
        spread_y(feat, z_block(step), step, fy_s, fy_r)
        forward(z_block(step))
        take_y(near(index - 1))
    take_y(near(nz - 1))

    loads[0].wait()

    def gather_rows(side, core):
        for index in range(nx):
            group = index * 2 + core

            @pl.when(group != w)
            def _():
                for j in range(ratio):
                    slot = group * ratio + j
                    arrived(xin.at[slot], fx_s.at[j], fx_r.at[slot])

            for j in range(ratio):
                lhs[side, pl.ds(index * rows, rows), pl.ds(j * cols, cols)] = (
                    xin[group * ratio + j].astype(jnp.float32) * gain_ref[w * ratio + j]
                ).astype(jnp.bfloat16)

    def project(side, kind):
        total = jnp.dot(lhs[side], qkv_w[kind], preferred_element_type=jnp.float32)
        return [total[at * rows : (at + 1) * rows] for at in range(nx)]

    def project_pair(kind):
        for at, term in enumerate(project(1, kind)):
            proj_send[at, kind] = term.astype(jnp.bfloat16)
            send(
                proj_send.at[at, kind], pair_in.at[at, kind],
                pair_s.at[at * 3 + kind], pair_r.at[at * 3 + kind], c, sibling_w,
            )

    def project_own(kind):
        for at, term in enumerate(project(0, kind)):
            proj_own[at, kind] = term

    def pass_on(kind):
        for at in range(nx):
            arrived(
                pair_in.at[at, kind], pair_s.at[at * 3 + kind], pair_r.at[at * 3 + kind]
            )
        for step in range(1, nx):
            at = up(x, step, nx)
            cross_send[step, kind] = (
                proj_own[at, kind] + pair_in[at, kind].astype(jnp.float32)
            ).astype(jnp.bfloat16)
            send(
                cross_send.at[step, kind], cross_in.at[step, kind],
                cross_s.at[step * 3 + kind], cross_r.at[step * 3 + kind], c, at * 2 + k,
            )

    gather_rows(1, other_k)
    project_pair(0)
    gather_rows(0, k)
    project_own(0)
    pass_on(0)
    project_pair(1)
    project_pair(2)

    squares = jnp.zeros((rows, 1), jnp.float32)
    for block in range(nc):
        wide = feat[block].astype(jnp.float32)
        squares += jnp.sum(wide * wide, axis=-1, keepdims=True)
    inverse = lax.rsqrt(squares / (nc * cols) + 1e-06)

    def projected(kind):
        total = proj_own[x, kind] + pair_in[x, kind].astype(jnp.float32)
        for step in range(1, nx):
            arrived(
                cross_in.at[step, kind], cross_s.at[step * 3 + kind], cross_r.at[step * 3 + kind]
            )
            total += cross_in[step, kind].astype(jnp.float32)
        return total * inverse

    def rotated(values):
        pieces = []
        for head in range(heads):
            piece = values[:, head * HEAD : (head + 1) * HEAD]
            pieces.append(piece * cos_ref[...] + pltpu.roll(piece, HEAD // 2, 1) * sin_ref[...])
        return jnp.concatenate(pieces, axis=1).astype(jnp.bfloat16)

    query_all[c] = rotated(projected(0))
    spread_y(query_all, c, 0, qy_s, qy_r)
    spread_z(query_all, qz_s, qz_r)
    for kind in (1, 2):
        project_own(kind)
        pass_on(kind)

    loads[3].wait()
    send(ow_all.at[w], ow_all.at[w], ow_s.at[0], ow_r.at[0], c, sibling_w)
    for step in range(1, nx):
        send(
            ow_all.at[w], ow_all.at[w], ow_s.at[step], ow_r.at[step],
            c, up(x, step, nx) * 2 + k,
        )

    def attend(query, keys, values, mask, meeting_mask):
        stat = jnp.zeros((rows, HEAD), jnp.float32)
        numers = []
        for head in range(heads):
            at = slice(head * HEAD, (head + 1) * HEAD)
            tops, totals, parts = [], [], []
            for m in range(meets):
                score = lax.dot_general(
                    query[m * new : (m + 1) * new, at], keys[m][:, at],
                    (((1,), (1,)), ((), ())), preferred_element_type=jnp.float32,
                ) * scale
                keep = mask[m] if meeting_mask else mask
                top = jnp.maximum(
                    jnp.max(jnp.where(keep, score, -jnp.inf), axis=-1, keepdims=True), FLOOR_SCORE
                )
                weight = jnp.where(keep, jnp.exp(score - top), 0.0)
                tops.append(top)
                totals.append(jnp.sum(weight, axis=-1, keepdims=True))
                parts.append(
                    jnp.dot(
                        weight.astype(jnp.bfloat16), values[m][:, at],
                        preferred_element_type=jnp.float32,
                    )
                )
            stat = jnp.where(lanes == head, jnp.concatenate(tops, axis=0), stat)
            stat = jnp.where(lanes == heads + head, jnp.concatenate(totals, axis=0), stat)
            numers.append(jnp.concatenate(parts, axis=0))
        return jnp.concatenate(numers, axis=1), stat

    loads[1].wait()
    loads[2].wait()

    cached = c * hist + lax.broadcasted_iota(jnp.int32, (new, hist), 1)

    def history(block):
        at = pl.ds(pl.multiple_of(block * cols, cols), cols)
        return attend(
            query_all[block],
            [k_mem[m, :, at] for m in range(meets)],
            [v_mem[m, :, at] for m in range(meets)],
            [cached < lengths_ref[m] for m in range(meets)], True,
        )

    def packed(stat):
        return jnp.transpose(stat)[: stat_send.shape[1]]

    def unpacked(short):
        filled = jnp.concatenate(
            [short, jnp.zeros((HEAD - short.shape[0], rows), jnp.float32)], axis=0
        )
        return jnp.transpose(filled)

    def merge(left, right):
        left_num, left_stat = left
        right_num, right_stat = right
        joint = jnp.maximum(left_stat, right_stat)
        left_scale = jnp.exp(left_stat - joint)
        right_scale = jnp.exp(right_stat - joint)
        stat = jnp.where(lanes < heads, joint, 0.0)
        pieces = []
        for head in range(heads):
            at = slice(head * HEAD, (head + 1) * HEAD)
            one, two = left_scale[:, head : head + 1], right_scale[:, head : head + 1]
            pieces.append(left_num[:, at] * one + right_num[:, at] * two)
            total = (
                left_stat[:, heads + head : heads + head + 1] * one
                + right_stat[:, heads + head : heads + head + 1] * two
            )
            stat = jnp.where(lanes == heads + head, total, stat)
        return jnp.concatenate(pieces, axis=1), stat

    @pl.loop(0, nz)
    def _(index):
        step = near(index)
        numer, stat = history(z_block(step))
        num_own[step] = numer
        stat_own[step] = stat

        @pl.when(index < nz - 1)
        def _():
            after = near(index + 1)
            ahead = z_block(after)
            arrived(query_all.at[ahead], qz_s.at[after], qz_r.at[after])
            remote(
                query_all.at[ahead], query_all.at[ahead], qy_s.at[after], qy_r.at[after],
                sibling_c, w,
            ).start()

        block = y_block(step)
        arrived(query_all.at[block], qy_s.at[step], qy_r.at[step])
        numer, stat = history(block)
        num_send[step] = numer.astype(jnp.bfloat16)
        stat_send[step] = packed(stat)
        remote(
            num_send.at[step], num_in.at[step], ny_s.at[step], ny_r.at[step], sibling_c, w
        ).start()
        remote(
            stat_send.at[step], stat_in.at[step], ty_s.at[step], ty_r.at[step], sibling_c, w
        ).start()

    for index in range(1, nz):
        step = near(index)
        block = z_block(step)
        arrived(num_in.at[step], ny_s.at[step], ny_r.at[step])
        arrived(stat_in.at[step], ty_s.at[step], ty_r.at[step])
        numer, stat = merge(
            (num_own[step], stat_own[step]),
            (num_in[step].astype(jnp.float32), unpacked(stat_in[step])),
        )
        num_cross_send[step] = numer.astype(jnp.bfloat16)
        stat_cross_send[step] = packed(stat)
        send(
            num_cross_send.at[step], num_cross_in.at[step], nz_s.at[step], nz_r.at[step],
            block, w,
        )
        send(
            stat_cross_send.at[step], stat_cross_in.at[step], tz_s.at[step], tz_r.at[step],
            block, w,
        )

    key_ref[...] = rotated(projected(1))
    value_ref[...] = projected(2).astype(jnp.bfloat16)

    causal = lax.broadcasted_iota(jnp.int32, (new, new), 0) >= lax.broadcasted_iota(
        jnp.int32, (new, new), 1
    )
    new_keys, new_values = key_ref[...], value_ref[...]
    numer, stat = attend(
        query_all[c],
        [new_keys[m * new : (m + 1) * new] for m in range(meets)],
        [new_values[m * new : (m + 1) * new] for m in range(meets)],
        causal, False,
    )
    arrived(num_in.at[0], ny_s.at[0], ny_r.at[0])
    arrived(stat_in.at[0], ty_s.at[0], ty_r.at[0])
    pair = merge(
        (num_own[0], stat_own[0]),
        (num_in[0].astype(jnp.float32), unpacked(stat_in[0])),
    )
    numer, stat = merge(pair, (numer, stat))
    num_own[0] = numer
    stat_own[0] = stat

    for step in range(1, nx):
        origin = down(x, step, nx) * 2 + k
        arrived(ow_all.at[origin], ow_s.at[step], ow_r.at[step])
        send(
            ow_all.at[origin], ow_all.at[origin], owf_s.at[step], owf_r.at[step], c, sibling_w
        )

    for step in range(1, nz):
        arrived(num_cross_in.at[step], nz_s.at[step], nz_r.at[step])
        arrived(stat_cross_in.at[step], tz_s.at[step], tz_r.at[step])
        numer, stat = merge(
            (num_own[0], stat_own[0]),
            (num_cross_in[step].astype(jnp.float32), unpacked(stat_cross_in[step])),
        )
        num_own[0] = numer
        stat_own[0] = stat
    stat = stat_own[0]
    for head in range(heads):
        at = slice(head * HEAD, (head + 1) * HEAD)
        attended[:, at] = (
            num_own[0, :, at] / stat[:, heads + head : heads + head + 1]
        ).astype(jnp.bfloat16)

    arrived(ow_all.at[sibling_w], ow_s.at[0], ow_r.at[0])
    for step in range(1, nx):
        origin = down(x, step, nx) * 2 + other_k
        arrived(ow_all.at[origin], owf_s.at[step], owf_r.at[step])

    def out_term(block):
        at = pl.ds(pl.multiple_of(lax.rem(block, ratio) * cols, cols), cols)
        return jnp.dot(
            attended[...], ow_all[lax.div(block, ratio), :, at],
            preferred_element_type=jnp.float32,
        )

    for index in range(nz):
        step = far(index)
        sum_send[step] = out_term(y_block(step)).astype(jnp.bfloat16)
        send(sum_send.at[step], sum_in.at[step], by_s.at[step], by_r.at[step], sibling_c, w)
    for index in range(nz):
        step = far(index)
        block = z_block(step)
        term = out_term(block)
        arrived(sum_in.at[step], by_s.at[step], by_r.at[step])
        term += sum_in[step].astype(jnp.float32)
        if index < nz - 1:
            sum_cross_send[step] = term.astype(jnp.bfloat16)
            send(
                sum_cross_send.at[step], sum_cross_in.at[step], bz_s.at[step], bz_r.at[step],
                block, w,
            )
        else:
            sum_own[...] = term

    total = sum_own[...]
    for step in range(1, nz):
        arrived(sum_cross_in.at[step], bz_s.at[step], bz_r.at[step])
        total += sum_cross_in[step].astype(jnp.float32)
    out_ref[...] = total.astype(jnp.bfloat16)

    def left(src, send_sem, recv_sem):
        remote(src, src, send_sem, recv_sem, sibling_c, w).wait_send()

    for copy in pending:
        copy.wait_send()
    for block in range(nc):
        target, _, copy = forward_copy(block)

        @pl.when(target != w)
        def _():
            copy.wait_send()

    for step in range(nz):
        left(num_send.at[step], ny_s.at[step], ny_r.at[step])
        left(stat_send.at[step], ty_s.at[step], ty_r.at[step])
        if step:
            left(query_all.at[z_block(step)], qy_s.at[step], qy_r.at[step])


def hand_out(first, second, third, one, two, three, sems):
    pairs = ((first, one), (second, two), (third, three))
    copies = [pltpu.make_async_copy(*pair, sems.at[i]) for i, pair in enumerate(pairs)]
    for copy in copies:
        copy.start()
    for copy in copies:
        copy.wait()


def shards(
    nc, nw,
    frames, span_source, adapter_weight, adapter_bias, norm_gain,
    qkv_weight, out_weight, k_cache, v_cache, lengths,
):
    rows, audio_width = frames.shape
    group_spans = span_source.shape[0]
    meets, hist, width = k_cache.shape
    depth, _, cols = qkv_weight.shape
    nz, nx = nc // LOW, nw // 2
    heads = cols // HEAD
    short = max(8, (2 * heads + 7) // 8 * 8)
    vmem = pl.BlockSpec(memory_space=pltpu.VMEM)
    smem = pl.BlockSpec(memory_space=pltpu.SMEM)
    anywhere = pl.BlockSpec(memory_space=pl.ANY)
    half_type, full_type = jnp.bfloat16, jnp.float32
    block = (rows, cols)
    dma = lambda count: pltpu.SemaphoreType.DMA((count,))
    result = jax.ShapeDtypeStruct(block, half_type)
    results = pl.pallas_call(
        functools.partial(layer_kernel, nc, nw, meets, hist),
        out_shape=(result, result, result),
        in_specs=[smem] * 2 + [anywhere] * 8,
        out_specs=(vmem, vmem, vmem),
        scratch_shapes=[
            pltpu.VMEM((group_spans, rows // group_spans, audio_width), half_type),
            pltpu.VMEM((audio_width, cols), half_type),
            pltpu.VMEM((1, cols), full_type),
            pltpu.VMEM((nc, 1, cols), full_type),
            pltpu.VMEM((rows, HEAD), full_type),
            pltpu.VMEM((rows, HEAD), full_type),
            pltpu.VMEM((2, nx * rows, depth), half_type),
            pltpu.VMEM((nc,) + block, half_type),
            pltpu.VMEM((nc,) + block, half_type),
            pltpu.VMEM((nc,) + block, half_type),
            pltpu.VMEM((3, depth, cols), half_type),
            pltpu.VMEM((meets, hist, width), half_type),
            pltpu.VMEM((meets, hist, width), half_type),
            pltpu.VMEM((nw,) + out_weight.shape, half_type),
            pltpu.VMEM((nx, 3) + block, full_type),
            pltpu.VMEM((nx, 3) + block, half_type),
            pltpu.VMEM((nx, 3) + block, half_type),
            pltpu.VMEM((nx, 3) + block, half_type),
            pltpu.VMEM((nx, 3) + block, half_type),
            pltpu.VMEM((nz,) + block, full_type),
            pltpu.VMEM((nz,) + block, half_type),
            pltpu.VMEM((nz,) + block, half_type),
            pltpu.VMEM((nz,) + block, half_type),
            pltpu.VMEM((nz,) + block, half_type),
            pltpu.VMEM((nz, rows, HEAD), full_type),
            pltpu.VMEM((nz, short, rows), full_type),
            pltpu.VMEM((nz, short, rows), full_type),
            pltpu.VMEM((nz, short, rows), full_type),
            pltpu.VMEM((nz, short, rows), full_type),
            pltpu.VMEM(block, full_type),
            pltpu.VMEM((nz,) + block, half_type),
            pltpu.VMEM((nz,) + block, half_type),
            pltpu.VMEM((nz,) + block, half_type),
            pltpu.VMEM((nz,) + block, half_type),
            pltpu.VMEM(block, half_type),
            dma(8),
            dma(nz), dma(nz), dma(nz), dma(nz), dma(nc), dma(nc),
            dma(3 * nx), dma(3 * nx), dma(3 * nx), dma(3 * nx),
            dma(nz), dma(nz), dma(nz), dma(nz),
            dma(nx), dma(nx), dma(nx), dma(nx),
            dma(nz), dma(nz), dma(nz), dma(nz), dma(nz), dma(nz), dma(nz), dma(nz),
            dma(nz), dma(nz), dma(nz), dma(nz),
        ],
        compiler_params=pltpu.CompilerParams(
            collective_id=0, has_side_effects=True, vmem_limit_bytes=60 * 1024 * 1024
        ),
        cost_estimate=pl.CostEstimate(
            flops=8 * rows * depth * 3 * cols,
            bytes_accessed=2 * (3 * depth * cols + 2 * meets * hist * width),
            transcendentals=0,
        ),
    )(
        span_source, lengths,
        frames.reshape(group_spans, rows // group_spans, audio_width), adapter_weight,
        adapter_bias.reshape(1, cols), norm_gain.reshape(nc, 1, cols),
        jnp.transpose(qkv_weight, (1, 0, 2)), out_weight, k_cache, v_cache,
    )
    return pl.pallas_call(
        hand_out,
        out_shape=(result, result, result),
        in_specs=[anywhere] * 3,
        out_specs=(anywhere,) * 3,
        scratch_shapes=[dma(3)],
        compiler_params=pltpu.CompilerParams(vmem_limit_bytes=60 * 1024 * 1024),
    )(*results)


def solution(mesh):
    nc, nw = mesh.shape["ctx"], mesh.shape["wt"]
    return jax.shard_map(
        functools.partial(shards, nc, nw),
        mesh=mesh,
        in_specs=(
            P("wt", None),
            P("wt"),
            P(None, "ctx"),
            P("ctx"),
            P(),
            P("wt", None, "ctx"),
            P("ctx", "wt"),
            P("wt", "ctx", None),
            P("wt", "ctx", None),
            P("wt"),
        ),
        out_specs=(P("wt", "ctx"), P("wt", "ctx"), P("wt", "ctx")),
        check_vma=False,
    )
```
